32 devices in a mesh: row: 8 (over y, x, core), col: 4 (over z).
Axes of the slice: x: 2, y: 2, z: 4, core: 2. Of those that a mesh axis runs over, the one named last changes fastest.
Arguments:
- tiles: bfloat16 [8192, 4096], P('row', 'col'), may hold values from -0.0625 to 0.0625
- block_map: int32 [8, 4, 8, 8], P('row', 'col'), may hold values from 0 to 1, as said below
- lanczos_block: bfloat16 [8, 8192], P(None, ('row', 'col')), may hold values from -6 to 6
Outputs:
- product: float32 [8, 8192], P(None, ('row', 'col'))
- projected: float32 [8, 8], replicated
The draws below stay inside these ranges and needn't reach their ends.
Inputs may be any that keep to these rules, and one draw needn't show every extreme that they name: `block_map`: 0 or 1; the share of nonzero sub-blocks differs from tile to tile.
All inputs are finite; a program needn't handle non-finite values.
Results may differ from the reference program's by a relative error of at most 0.0003.
Values may be sent and summed in bfloat16 or wider, within the bound.
No kernel may reach another device: no remote copies, remote signals or barrier semaphores. Data moves between devices by JAX's collectives and lax.ppermute only.
A program may use at most 64 MiB of HBM per device.

```python
import jax
import jax.numpy as jnp
from jax import lax

BR = 1024
SUB = 128
KVEC = 8
SB = 8
NTOT = 8192
N_ROW = 8
N_COL = 4


def draw_block_map(key, part):
    dense_key = jax.random.fold_in(key, 11)
    pick_key = jax.random.fold_in(key, 23)
    density = jax.random.randint(dense_key, (N_ROW, N_COL, 1, 1), 1, 9)
    picks = jax.random.randint(pick_key, (N_ROW, N_COL, SB, SB), 0, 8)
    return (picks < density).astype(jnp.int32)


def level_of(stream_key, shape, split, low, high):
    def one(position, shards_of):
        steps = jax.random.uniform(jax.random.fold_in(jax.random.fold_in(stream_key, 6), position), (shards_of,), jnp.float32, low / len(split), high / len(split))
        return jnp.repeat(jnp.exp(steps), shape[position] // shards_of).reshape((-1,) + (1,) * (len(shape) - position - 1))

    gain = one(*split[0])
    for cut in split[1:]:
        gain = gain * one(*cut)
    return gain


def scatter_about(rng, dims, deviation, limit, cuts=(), held_as=jnp.bfloat16):
    array = deviation * jax.random.normal(rng, dims, jnp.float32)
    if cuts:
        array = array * level_of(rng, dims, cuts, -0.22, 0.18)
    return jnp.clip(array, -limit, limit).astype(held_as)


def setup_inputs(seed: int = 0) -> dict:
    key_of = jax.random.split(jax.random.key(seed), 4)
    return {
        "tiles": scatter_about(key_of[0], (NTOT, N_COL * BR), (2 * BR * N_COL) ** -0.5, 0.0625, ((0, 8), (1, 4))),
        "block_map": draw_block_map(jax.random.fold_in(key_of[3], 71), 0),
        "lanczos_block": scatter_about(key_of[2], (KVEC, NTOT), 1.0, 6.0, ((1, 32),)),
    }


def masked_tile(tiles, block_map, row_idx, offset):
    tile = tiles[row_idx * BR:(row_idx + 1) * BR, offset * BR:(offset + 1) * BR]
    keep = block_map[row_idx, offset].astype(jnp.bfloat16)
    shaped = tile.reshape(SB, SUB, SB, SUB) * keep[:, None, :, None]
    return shaped.reshape(BR, BR)

def reference(tiles, block_map, lanczos_block):
    product = jnp.zeros((KVEC, NTOT), jnp.float32)
    for row_idx in range(N_ROW):
        source = lanczos_block[:, row_idx * BR:(row_idx + 1) * BR]
        for offset in range(min(N_COL, N_ROW - row_idx)):
            target = row_idx + offset
            matrix = masked_tile(tiles, block_map, row_idx, offset)
            far_vec = lanczos_block[:, target * BR:(target + 1) * BR]
            plain = lax.dot_general(far_vec, matrix, (((1,), (1,)), ((), ())), preferred_element_type=jnp.float32)
            mirror = jnp.dot(source, matrix, preferred_element_type=jnp.float32)
            product = product.at[:, row_idx * BR:(row_idx + 1) * BR].add(plain)
            product = product.at[:, target * BR:(target + 1) * BR].add(mirror)
    inner = jnp.dot(lanczos_block.astype(jnp.float32), product.T, precision=lax.Precision.HIGHEST)
    projected = inner * (1.0 / jnp.sqrt(jnp.float32(NTOT)))
    return (product, projected)
```

```python
import jax
import jax.numpy as jnp
from jax import lax
from jax.sharding import PartitionSpec as P

SUB = 128
AXES = ("row", "col")


def bits_of(axis):
    return range(lax.axis_size(axis).bit_length() - 1)


def route(target):
    rows, cols = lax.axis_size("row"), lax.axis_size("col")
    pairs = []
    for r in range(rows):
        for c in range(cols):
            to_row, to_col = target(r, c)
            if 0 <= to_row < rows:
                pairs.append((r * cols + c, to_row * cols + to_col))
    return pairs


def across_row(block, bit):
    return lax.ppermute(block, AXES, route(lambda r, c: (r ^ (1 << bit), c)))


def across_col(block, bit):
    return lax.ppermute(block, AXES, route(lambda r, c: (r, c ^ (1 << bit))))


def from_far(block):
    return lax.ppermute(block, AXES, route(lambda r, c: (r - c, c)))


def to_far(block):
    return lax.ppermute(block, AXES, route(lambda r, c: (r + c, c)))


def on_device(tiles, block_map, lanczos_block):
    width = tiles.shape[0]
    vectors = lanczos_block.shape[0]
    groups = width // SUB
    col_idx = lax.axis_index("col")
    total = width * lax.axis_size("row")

    keep = block_map[0, 0].astype(jnp.bfloat16)
    matrix = (tiles.reshape(groups, SUB, groups, SUB) * keep[:, None, :, None]).reshape(
        width, width
    )

    source = lanczos_block
    for bit in bits_of("col"):
        other = across_col(source, bit)
        upper = (col_idx >> bit) % 2 == 1
        source = jnp.concatenate(
            [jnp.where(upper, other, source), jnp.where(upper, source, other)], axis=1
        )
    far_vec = from_far(source)
    mirror = jnp.dot(source, matrix, preferred_element_type=jnp.float32)
    arrived = to_far(mirror)
    plain = lax.dot_general(
        far_vec, matrix, (((1,), (1,)), ((), ())), preferred_element_type=jnp.float32
    )
    gram = lax.dot_general(
        mirror,
        far_vec.astype(jnp.float32),
        (((1,), (1,)), ((), ())),
        precision=lax.Precision.HIGHEST,
    )
    for bit in bits_of("row"):
        gram = gram + across_row(gram, bit)
    gram = jnp.pad(gram, ((0, 0), (0, SUB - vectors)))
    sums = plain + arrived
    for bit in reversed(bits_of("col")):
        half = sums.shape[1] // 2
        upper = (col_idx >> bit) % 2 == 1
        given = jnp.where(upper, sums[:, :half], sums[:, half:])
        kept = jnp.where(upper, sums[:, half:], sums[:, :half])
        other = across_col(jnp.concatenate([given, gram], axis=1), bit)
        sums = kept + other[:, :half]
        gram = gram + other[:, half:]
    gram = gram[:, :vectors]
    projected = (gram + gram.T) * (1.0 / jnp.sqrt(jnp.float32(total)))
    return (sums, projected)


def solution(mesh):
    placed = (P("row", "col"), P("row", "col", None, None), P(None, ("row", "col")))
    return jax.shard_map(
        on_device,
        mesh=mesh,
        in_specs=placed,
        out_specs=(P(None, ("row", "col")), P()),
        check_vma=False,
    )
```

```python
import jax
import jax.numpy as jnp
from jax import lax
from jax.sharding import PartitionSpec as P

SUB = 128
AXES = ("row", "col")


def bits_of(axis):
    return range(lax.axis_size(axis).bit_length() - 1)


def send(block, target):
    rows, cols = lax.axis_size("row"), lax.axis_size("col")
    pairs = []
    for r in range(rows):
        for c in range(cols):
            to_row, to_col = target(r, c)
            pairs.append((r * cols + c, (to_row % rows) * cols + to_col))
    return lax.ppermute(block, AXES, pairs)


def across_row(block, bit):
    return send(block, lambda r, c: (r ^ (1 << bit) ^ (1 if bit else 0), c))


def across_col(block, bit):
    return send(block, lambda r, c: (r, c ^ (1 << bit)))


def from_far(block):
    return send(block, lambda r, c: (r - c if c else r ^ 1, c))


def to_far(block):
    return send(block, lambda r, c: (r + c if c else r ^ 1, c))


def on_device(tiles, block_map, lanczos_block):
    width = tiles.shape[0]
    vectors = lanczos_block.shape[0]
    groups = width // SUB
    rows = lax.axis_size("row")
    row_idx = lax.axis_index("row")
    col_idx = lax.axis_index("col")

    keep = block_map[0, 0].astype(jnp.bfloat16)
    matrix = (tiles.reshape(groups, SUB, groups, SUB) * keep[:, None, :, None]).reshape(
        width, width
    )

    source = lanczos_block
    for bit in bits_of("col"):
        other = across_col(source, bit)
        upper = (col_idx >> bit) % 2 == 1
        zero = jnp.zeros_like(source)
        low, high = jnp.where(upper, zero, source), jnp.where(upper, source, zero)
        if bit == 0:
            low, high = lax.optimization_barrier((low, high))
        source = jnp.concatenate(
            [jnp.where(upper, other, low), jnp.where(upper, high, other)], axis=1
        )
    far_vec = from_far(source)
    mirror = jnp.dot(source, matrix, preferred_element_type=jnp.float32)
    arrived = to_far(mirror)
    inside = row_idx + col_idx < rows
    far_vec = jnp.where(inside, far_vec, jnp.zeros_like(far_vec))
    far_vec = jnp.where(col_idx == 0, source, far_vec)
    gram = lax.dot_general(
        mirror,
        far_vec.astype(jnp.float32),
        (((1,), (1,)), ((), ())),
        precision=lax.Precision.HIGHEST,
    )
    plain = lax.dot_general(
        far_vec, matrix, (((1,), (1,)), ((), ())), preferred_element_type=jnp.float32
    )
    for bit in bits_of("row"):
        gram = gram + across_row(gram, bit)
        if bit == 1:
            gram, plain = lax.optimization_barrier((gram, plain))
    gram = jnp.pad(gram, ((0, 0), (0, SUB - vectors)))
    arrived = jnp.where(row_idx >= col_idx, arrived, jnp.zeros_like(arrived))
    arrived = jnp.where(col_idx == 0, mirror, arrived)
    sums = plain + arrived
    for bit in reversed(bits_of("col")):
        half = sums.shape[1] // 2
        upper = (col_idx >> bit) % 2 == 1
        given = jnp.where(upper, sums[:, :half], sums[:, half:])
        kept = jnp.where(upper, sums[:, half:], sums[:, :half])
        other = across_col(jnp.concatenate([given, gram], axis=1), bit)
        sums = kept + other[:, :half]
        gram = gram + other[:, half:]
    gram = gram[:, :vectors]
    projected = (gram + gram.T) * (1.0 / jnp.sqrt(jnp.float32(width * rows)))
    return (sums, projected)


def solution(mesh):
    placed = (P("row", "col"), P("row", "col", None, None), P(None, ("row", "col")))
    return jax.shard_map(
        on_device,
        mesh=mesh,
        in_specs=placed,
        out_specs=(P(None, ("row", "col")), P()),
        check_vma=False,
    )
```

```python
import jax
import jax.numpy as jnp
from jax import lax
from jax.sharding import PartitionSpec as P

SUB = 128
AXES = ("row", "col")


def send(block, target):
    rows, cols = lax.axis_size("row"), lax.axis_size("col")
    pairs = []
    for r in range(rows):
        for c in range(cols):
            to_row, to_col = target(r, c)
            pairs.append((r * cols + c, (to_row % rows) * cols + to_col))
    return lax.ppermute(block, AXES, pairs)


def across_row(block, mask):
    return send(block, lambda r, c: (r ^ mask, c))


def across_col(block, mask):
    return send(block, lambda r, c: (r, c ^ mask))


def from_far(block):
    return send(block, lambda r, c: (r - c if c else r ^ 1, c))


def to_far(block):
    return send(block, lambda r, c: (r + c if c else r ^ 1, c))


def groups_of(first, last):
    return [(bit, 4 if bit + 1 < last else 2) for bit in range(first, last, 2)]


def choose(place, blocks):
    chosen = blocks[-1]
    for k in reversed(range(len(blocks) - 1)):
        chosen = jnp.where(place == k, blocks[k], chosen)
    return chosen


def tree_sum(blocks):
    while len(blocks) > 1:
        blocks = [a + b for a, b in zip(blocks[::2], blocks[1::2])]
    return blocks[0]


def on_device(tiles, block_map, lanczos_block):
    width = tiles.shape[0]
    vectors = lanczos_block.shape[0]
    parts = width // SUB
    rows, cols = lax.axis_size("row"), lax.axis_size("col")
    row_idx = lax.axis_index("row")
    col_idx = lax.axis_index("col")
    row_bits, col_bits = rows.bit_length() - 1, cols.bit_length() - 1

    keep = block_map[0, 0].astype(jnp.bfloat16)
    matrix = (tiles.reshape(parts, SUB, parts, SUB) * keep[:, None, :, None]).reshape(
        width, width
    )

    source = lanczos_block
    for bit, members in groups_of(0, col_bits):
        place = (col_idx >> bit) % members
        got = {k: across_col(source, k << bit) for k in reversed(range(1, members))}
        if members == 4:
            vals = lax.optimization_barrier(tuple(got[k] for k in (2, 3, 1)))
            got = dict(zip((2, 3, 1), vals))
        placed = jnp.concatenate(
            [
                jnp.where(place == at, source, jnp.zeros_like(source))
                for at in range(members)
            ],
            axis=1,
        )
        if bit == 0:
            placed = lax.optimization_barrier(placed)
        got[0] = jnp.zeros_like(source)
        source = placed + jnp.concatenate(
            [
                choose(place, [got[at ^ k] for k in range(members)])
                for at in range(members)
            ],
            axis=1,
        )
    far_vec = from_far(source)
    mirror = jnp.dot(source, matrix, preferred_element_type=jnp.float32)
    inside = row_idx + col_idx < rows
    far_vec = jnp.where(inside, far_vec, jnp.zeros_like(far_vec))
    far_vec = jnp.where(col_idx == 0, source, far_vec)
    gram = lax.dot_general(
        mirror,
        far_vec.astype(jnp.float32),
        (((1,), (1,)), ((), ())),
        precision=lax.Precision.HIGHEST,
    )
    plain = lax.dot_general(
        far_vec, matrix, (((1,), (1,)), ((), ())), preferred_element_type=jnp.float32
    )
    gram = gram + across_row(gram, 1)
    gram, plain = lax.optimization_barrier((gram, plain))
    arrived = to_far(mirror)
    for bit, members in groups_of(1, row_bits):
        got = {k: across_row(gram, k << bit | 1) for k in reversed(range(1, members))}
        if bit == 1 and 1 in got:
            got[1], arrived = lax.optimization_barrier((got[1], arrived))
        gram = tree_sum([gram] + [got[k] for k in range(1, members)])
    gram = jnp.pad(gram, ((0, 0), (0, SUB - vectors)))
    arrived = jnp.where(row_idx >= col_idx, arrived, jnp.zeros_like(arrived))
    arrived = jnp.where(col_idx == 0, mirror, arrived)
    sums = plain + arrived
    for bit, members in reversed(groups_of(0, col_bits)):
        place = (col_idx >> bit) % members
        pieces = jnp.split(sums, members, axis=1)
        given = {
            k: jnp.concatenate(
                [choose(place, [pieces[at ^ k] for at in range(members)]), gram], axis=1
            )
            for k in range(1, members)
        }
        got = {k: across_col(given[k], k << bit) for k in reversed(range(1, members))}
        own = jnp.concatenate([choose(place, pieces), gram], axis=1)
        others = (2, 1, 3) if members == 4 else (1,)
        both = tree_sum([own] + [got[k] for k in others])
        sums, gram = both[:, : -SUB], both[:, -SUB:]
    gram = gram[:, :vectors]
    projected = (gram + gram.T) * (1.0 / jnp.sqrt(jnp.float32(width * rows)))
    return (sums, projected)


def solution(mesh):
    placed = (P("row", "col"), P("row", "col", None, None), P(None, ("row", "col")))
    return jax.shard_map(
        on_device,
        mesh=mesh,
        in_specs=placed,
        out_specs=(P(None, ("row", "col")), P()),
        check_vma=False,
    )
```

```python
import functools

import jax
import jax.numpy as jnp
from jax import lax
from jax.experimental import pallas as pl
from jax.experimental.pallas import tpu as pltpu
from jax.sharding import PartitionSpec as P

SUB = 128
AXES = ("row", "col")
ONE = ((1, 0),)
ROW_TABLES = ((1, 0, 3, 2), (2, 3, 0, 1), (3, 2, 1, 0))
ROW_ORDER = (0, 1, 2)
GATHER_TABLES = ((1, 0, 3, 2), (2, 3, 0, 1), (3, 2, 1, 0))
GATHER_ORDER = (1, 2, 0)
SUM_TABLES = ((1, 3, 0, 2), (3, 2, 1, 0), (2, 0, 3, 1))
SUM_ORDER = (1, 2, 0)


def send(block, target):
    rows, cols = lax.axis_size("row"), lax.axis_size("col")
    pairs = []
    for r in range(rows):
        for c in range(cols):
            to_row, to_col = target(r, c)
            pairs.append((r * cols + c, (to_row % rows) * cols + to_col))
    return lax.ppermute(block, AXES, pairs)


def moved(index, bit, table):
    size = len(table) - 1
    return index & ~(size << bit) | table[index >> bit & size] << bit


def exchanged(blocks, bit, tables, axis):
    if axis == "row":
        goes = [lambda r, c, t=t: (moved(r, bit, t) ^ 1, c) for t in tables]
    else:
        goes = [lambda r, c, t=t: (r, moved(c, bit, t)) for t in tables]
    return [send(block, to) for block, to in zip(blocks, goes)]


def held(blocks, order):
    if len(blocks) != len(order):
        return blocks
    kept = lax.optimization_barrier(tuple(blocks[k] for k in order))
    return [kept[order.index(k)] for k in range(len(blocks))]


def from_far(block):
    return send(block, lambda r, c: (r - c if c else r ^ 1, c))


def to_far(block):
    return send(block, lambda r, c: (r + c if c else r ^ 1, c))


def groups_of(first, last):
    return [(bit, 4 if bit + 1 < last else 2) for bit in range(first, last, 2)]


def choose(place, blocks):
    chosen = blocks[-1]
    for k in reversed(range(len(blocks) - 1)):
        chosen = jnp.where(place == k, blocks[k], chosen)
    return chosen


def in_place(own, got, tables, place):
    members = len(tables) + 1

    def source(d, k):
        return next(g for g, t in zip(got, tables) if t[d ^ k] == d)

    return [own] + [
        choose(place, [source(d, k) for d in range(members)]) for k in range(1, members)
    ]


def tree_sum(blocks):
    while len(blocks) > 1:
        blocks = [a + b for a, b in zip(blocks[::2], blocks[1::2])]
    return blocks[0]


def write_results(scale, both_ref, product_ref, projected_ref):
    vectors = projected_ref.shape[0]
    product_ref[...] = both_ref[:, :-SUB]
    gram = both_ref[:, -SUB:]
    square = jnp.concatenate([gram, jnp.zeros((SUB - vectors, SUB), jnp.float32)])
    gram = gram + square.T[:vectors]
    projected_ref[...] = (gram * scale)[:, :vectors]


def on_device(tiles, block_map, lanczos_block):
    width = tiles.shape[0]
    vectors = lanczos_block.shape[0]
    parts = width // SUB
    rows, cols = lax.axis_size("row"), lax.axis_size("col")
    row_idx = lax.axis_index("row")
    col_idx = lax.axis_index("col")
    row_bits, col_bits = rows.bit_length() - 1, cols.bit_length() - 1

    keep = block_map[0, 0].astype(jnp.bfloat16)
    matrix = (tiles.reshape(parts, SUB, parts, SUB) * keep[:, None, :, None]).reshape(
        width, width
    )

    source = lanczos_block
    for bit, members in groups_of(0, col_bits):
        place = (col_idx >> bit) % members
        tables = GATHER_TABLES if members == 4 else ONE
        got = held(
            exchanged([source] * len(tables), bit, tables, "col"), GATHER_ORDER
        )
        zero = jnp.zeros_like(source)
        placed = jnp.concatenate(
            [jnp.where(place == at, source, zero) for at in range(members)], axis=1
        )
        if bit == 0:
            placed = lax.optimization_barrier(placed)
        others = in_place(zero, got, tables, place)
        source = placed + jnp.concatenate(
            [
                choose(place, [others[at ^ d] for d in range(members)])
                for at in range(members)
            ],
            axis=1,
        )

    far_vec = from_far(source)
    mirror = jnp.dot(source, matrix, preferred_element_type=jnp.float32)
    inside = row_idx + col_idx < rows
    far_vec = jnp.where(inside, far_vec, jnp.zeros_like(far_vec))
    far_vec = jnp.where(col_idx == 0, source, far_vec)
    gram = lax.dot_general(
        mirror,
        far_vec.astype(jnp.float32),
        (((1,), (1,)), ((), ())),
        precision=lax.Precision.HIGHEST,
    )
    plain = lax.dot_general(
        far_vec, matrix, (((1,), (1,)), ((), ())), preferred_element_type=jnp.float32
    )

    gram = gram + send(gram, lambda r, c: (r ^ 1, c))
    gram, plain = lax.optimization_barrier((gram, plain))
    arrived = to_far(mirror)
    for bit, members in groups_of(1, row_bits):
        place = (row_idx >> bit) % members
        tables = ROW_TABLES if members == 4 else ONE
        got = exchanged([gram] * len(tables), bit, tables, "row")
        if bit == 1:
            got[0], arrived = lax.optimization_barrier((got[0], arrived))
        gram = tree_sum(in_place(gram, held(got, ROW_ORDER), tables, place))

    gram = jnp.pad(gram, ((0, 0), (0, SUB - vectors)))
    arrived = jnp.where(row_idx >= col_idx, arrived, jnp.zeros_like(arrived))
    arrived = jnp.where(col_idx == 0, mirror, arrived)
    both = jnp.concatenate([plain + arrived, gram], axis=1)
    for bit, members in reversed(groups_of(0, col_bits)):
        place = (col_idx >> bit) % members
        tables = SUM_TABLES if members == 4 else ONE
        pieces = jnp.split(both[:, :-SUB], members, axis=1)
        gram = both[:, -SUB:]
        given = [
            jnp.concatenate([choose(place, [pieces[to] for to in table]), gram], axis=1)
            for table in tables
        ]
        own = jnp.concatenate([choose(place, pieces), gram], axis=1)
        got = held(exchanged(given, bit, tables, "col"), SUM_ORDER)
        both = tree_sum(in_place(own, got, tables, place))

    return pl.pallas_call(
        functools.partial(write_results, 1.0 / (width * rows) ** 0.5),
        out_shape=(
            jax.ShapeDtypeStruct(lanczos_block.shape, jnp.float32),
            jax.ShapeDtypeStruct((vectors, vectors), jnp.float32),
        ),
        in_specs=[pl.BlockSpec(memory_space=pltpu.VMEM)],
        out_specs=(pl.BlockSpec(memory_space=pltpu.VMEM),) * 2,
        compiler_params=pltpu.CompilerParams(vmem_limit_bytes=1 << 20),
    )(both)


def solution(mesh):
    placed = (P("row", "col"), P("row", "col", None, None), P(None, ("row", "col")))
    return jax.shard_map(
        on_device,
        mesh=mesh,
        in_specs=placed,
        out_specs=(P(None, ("row", "col")), P()),
        check_vma=False,
    )
```

```python
import functools

import jax
import jax.numpy as jnp
from jax import lax
from jax.experimental import pallas as pl
from jax.experimental.pallas import tpu as pltpu
from jax.sharding import PartitionSpec as P

SUB = 128
AXES = ("row", "col")
ONE = ((1, 0),)
ROW_TABLES = ((2, 1, 0, 3), (1, 2, 3, 0), (3, 0, 1, 2), (0, 3, 2, 1))
ROW_ORDER = (0, 2, 3, 1)
GATHER_TABLES = ((2, 0, 3, 1), (0, 2, 1, 3), (3, 1, 0, 2), (1, 3, 2, 0))
GATHER_ORDER = (0, 1, 2, 3)
SUM_TABLES = ((1, 3, 2, 0), (2, 1, 0, 3), (3, 0, 1, 2), (0, 2, 3, 1))
SUM_ORDER = (0, 1, 2, 3)


def send(block, target):
    rows, cols = lax.axis_size("row"), lax.axis_size("col")
    pairs = []
    for r in range(rows):
        for c in range(cols):
            to_row, to_col = target(r, c)
            pairs.append((r * cols + c, (to_row % rows) * cols + to_col))
    return lax.ppermute(block, AXES, pairs)


def moved(index, bit, table):
    size = len(table) - 1
    return index & ~(size << bit) | table[index >> bit & size] << bit


def exchanged(blocks, bit, tables, axis):
    if axis == "row":
        goes = [lambda r, c, t=t: (moved(r, bit, t) ^ 1, c) for t in tables]
    else:
        goes = [
            lambda r, c, t=t: (r ^ (moved(c, bit, t) == c), moved(c, bit, t))
            for t in tables
        ]
    return [send(block, to) for block, to in zip(blocks, goes)]


def held(blocks, order):
    if len(blocks) != len(order):
        return blocks
    kept = lax.optimization_barrier(tuple(blocks[k] for k in order))
    return [kept[order.index(k)] for k in range(len(blocks))]


def from_far(block):
    return send(block, lambda r, c: (r - c if c else r ^ 1, c))


def to_far(block):
    return send(block, lambda r, c: (r + c if c else r ^ 1, c))


def groups_of(first, last):
    return [(bit, 4 if bit + 1 < last else 2) for bit in range(first, last, 2)]


def choose(place, blocks):
    chosen = blocks[-1]
    for k in reversed(range(len(blocks) - 1)):
        chosen = jnp.where(place == k, blocks[k], chosen)
    return chosen


def in_place(own, got, tables, place):
    members = len(tables[0])

    def source(d, k):
        return next(g for g, t in zip(got, tables) if t[d ^ k] == d)

    return [own] + [
        choose(place, [source(d, k) for d in range(members)]) for k in range(1, members)
    ]


def tree_sum(blocks):
    while len(blocks) > 1:
        blocks = [a + b for a, b in zip(blocks[::2], blocks[1::2])]
    return blocks[0]


def write_results(scale, both_ref, product_ref, projected_ref):
    vectors = projected_ref.shape[0]
    product_ref[...] = both_ref[:, :-SUB]
    gram = both_ref[:, -SUB:]
    square = jnp.concatenate([gram, jnp.zeros((SUB - vectors, SUB), jnp.float32)])
    gram = gram + square.T[:vectors]
    projected_ref[...] = (gram * scale)[:, :vectors]


def on_device(tiles, block_map, lanczos_block):
    width = tiles.shape[0]
    vectors = lanczos_block.shape[0]
    parts = width // SUB
    rows, cols = lax.axis_size("row"), lax.axis_size("col")
    row_idx = lax.axis_index("row")
    col_idx = lax.axis_index("col")
    row_bits, col_bits = rows.bit_length() - 1, cols.bit_length() - 1

    keep = block_map[0, 0].astype(jnp.bfloat16)
    matrix = (tiles.reshape(parts, SUB, parts, SUB) * keep[:, None, :, None]).reshape(
        width, width
    )

    source = lanczos_block
    for bit, members in groups_of(0, col_bits):
        place = (col_idx >> bit) % members
        tables = GATHER_TABLES if members == 4 else ONE
        got = held(
            exchanged([source] * len(tables), bit, tables, "col"), GATHER_ORDER
        )
        zero = jnp.zeros_like(source)
        placed = jnp.concatenate(
            [jnp.where(place == at, source, zero) for at in range(members)], axis=1
        )
        if bit == 0:
            placed = lax.optimization_barrier(placed)
        others = in_place(zero, got, tables, place)
        source = placed + jnp.concatenate(
            [
                choose(place, [others[at ^ d] for d in range(members)])
                for at in range(members)
            ],
            axis=1,
        )

    far_vec = from_far(source)
    mirror = jnp.dot(source, matrix, preferred_element_type=jnp.float32)
    inside = row_idx + col_idx < rows
    far_vec = jnp.where(inside, far_vec, jnp.zeros_like(far_vec))
    far_vec = jnp.where(col_idx == 0, source, far_vec)
    gram = lax.dot_general(
        mirror,
        far_vec.astype(jnp.float32),
        (((1,), (1,)), ((), ())),
        precision=lax.Precision.HIGHEST,
    )
    plain = lax.dot_general(
        far_vec, matrix, (((1,), (1,)), ((), ())), preferred_element_type=jnp.float32
    )

    gram = gram + send(gram, lambda r, c: (r ^ 1, c))
    gram, plain = lax.optimization_barrier((gram, plain))
    arrived = to_far(mirror)
    for bit, members in groups_of(1, row_bits):
        place = (row_idx >> bit) % members
        tables = ROW_TABLES if members == 4 else ONE
        got = exchanged([gram] * len(tables), bit, tables, "row")
        if bit == 1:
            got[0], arrived = lax.optimization_barrier((got[0], arrived))
        gram = tree_sum(in_place(gram, held(got, ROW_ORDER), tables, place))

    gram = jnp.pad(gram, ((0, 0), (0, SUB - vectors)))
    arrived = jnp.where(row_idx >= col_idx, arrived, jnp.zeros_like(arrived))
    arrived = jnp.where(col_idx == 0, mirror, arrived)
    both = jnp.concatenate([plain + arrived, gram], axis=1)
    for bit, members in reversed(groups_of(0, col_bits)):
        place = (col_idx >> bit) % members
        tables = SUM_TABLES if members == 4 else ONE
        pieces = jnp.split(both[:, :-SUB], members, axis=1)
        gram = both[:, -SUB:]
        given = [
            jnp.concatenate([choose(place, [pieces[to] for to in table]), gram], axis=1)
            for table in tables
        ]
        own = jnp.concatenate([choose(place, pieces), gram], axis=1)
        got = held(exchanged(given, bit, tables, "col"), SUM_ORDER)
        both = tree_sum(in_place(own, got, tables, place))

    return pl.pallas_call(
        functools.partial(write_results, 1.0 / (width * rows) ** 0.5),
        out_shape=(
            jax.ShapeDtypeStruct(lanczos_block.shape, jnp.float32),
            jax.ShapeDtypeStruct((vectors, vectors), jnp.float32),
        ),
        in_specs=[pl.BlockSpec(memory_space=pltpu.VMEM)],
        out_specs=(pl.BlockSpec(memory_space=pltpu.VMEM),) * 2,
        compiler_params=pltpu.CompilerParams(vmem_limit_bytes=1 << 20),
    )(both)


def solution(mesh):
    placed = (P("row", "col"), P("row", "col", None, None), P(None, ("row", "col")))
    return jax.shard_map(
        on_device,
        mesh=mesh,
        in_specs=placed,
        out_specs=(P(None, ("row", "col")), P()),
        check_vma=False,
    )
```

```python
import functools

import jax
import jax.numpy as jnp
from jax import lax
from jax.experimental import pallas as pl
from jax.experimental.pallas import tpu as pltpu
from jax.sharding import PartitionSpec as P

SUB = 128
AXES = ("row", "col")
ONE = ((1, 0),)
ROW_TABLES = ((2, 1, 0, 3), (1, 2, 3, 0), (3, 0, 1, 2), (0, 3, 2, 1))
ROW_ORDER = (0, 2, 3, 1)
GATHER_TABLES = ((2, 3, 0, 1), (0, 1, 3, 2), (3, 2, 1, 0), (1, 0, 2, 3))
GATHER_ORDER = (0, 1, 2, 3)
SUM_TABLES = ((1, 3, 2, 0), (2, 1, 0, 3), (3, 0, 1, 2), (0, 2, 3, 1))
SUM_ORDER = (0, 1, 2, 3)


def send(block, target):
    rows, cols = lax.axis_size("row"), lax.axis_size("col")
    pairs = []
    for r in range(rows):
        for c in range(cols):
            to_row, to_col = target(r, c)
            pairs.append((r * cols + c, (to_row % rows) * cols + to_col))
    return lax.ppermute(block, AXES, pairs)


def moved(index, bit, table):
    size = len(table) - 1
    return index & ~(size << bit) | table[index >> bit & size] << bit


def exchanged(blocks, bit, tables, axis):
    if axis == "row":
        goes = [lambda r, c, t=t: (moved(r, bit, t) ^ 1, c) for t in tables]
    elif axis == "cross":
        goes = [lambda r, c, t=t: (r ^ 1, moved(c, bit, t)) for t in tables]
    else:
        goes = [
            lambda r, c, t=t: (r ^ (moved(c, bit, t) == c), moved(c, bit, t))
            for t in tables
        ]
    return [send(block, to) for block, to in zip(blocks, goes)]


def held(blocks, order):
    if len(blocks) != len(order):
        return blocks
    kept = lax.optimization_barrier(tuple(blocks[k] for k in order))
    return [kept[order.index(k)] for k in range(len(blocks))]


def from_far(block):
    return send(block, lambda r, c: (r - c if c else r ^ 1, c))


def to_far(block):
    return send(block, lambda r, c: (r + c if c else r ^ 1, c))


def groups_of(first, last):
    return [(bit, 4 if bit + 1 < last else 2) for bit in range(first, last, 2)]


def choose(place, blocks):
    chosen = blocks[-1]
    for k in reversed(range(len(blocks) - 1)):
        chosen = jnp.where(place == k, blocks[k], chosen)
    return chosen


def in_place(own, got, tables, place):
    members = len(tables[0])

    def source(d, k):
        return next(g for g, t in zip(got, tables) if t[d ^ k] == d)

    return [own] + [
        choose(place, [source(d, k) for d in range(members)]) for k in range(1, members)
    ]


def tree_sum(blocks):
    while len(blocks) > 1:
        blocks = [a + b for a, b in zip(blocks[::2], blocks[1::2])]
    return blocks[0]


def write_results(scale, both_ref, product_ref, projected_ref):
    vectors = projected_ref.shape[0]
    product_ref[...] = both_ref[:, :-SUB]
    gram = both_ref[:, -SUB:]
    square = jnp.concatenate([gram, jnp.zeros((SUB - vectors, SUB), jnp.float32)])
    gram = gram + square.T[:vectors]
    projected_ref[...] = (gram * scale)[:, :vectors]


def on_device(tiles, block_map, lanczos_block):
    width = tiles.shape[0]
    vectors = lanczos_block.shape[0]
    parts = width // SUB
    rows, cols = lax.axis_size("row"), lax.axis_size("col")
    row_idx = lax.axis_index("row")
    col_idx = lax.axis_index("col")
    row_bits, col_bits = rows.bit_length() - 1, cols.bit_length() - 1

    keep = block_map[0, 0].astype(jnp.bfloat16)
    matrix = (tiles.reshape(parts, SUB, parts, SUB) * keep[:, None, :, None]).reshape(
        width, width
    )

    source = lanczos_block
    for bit, members in groups_of(0, col_bits):
        place = (col_idx >> bit) % members
        tables = GATHER_TABLES if members == 4 else ONE
        got = held(
            exchanged([source] * len(tables), bit, tables, "col"), GATHER_ORDER
        )
        zero = jnp.zeros_like(source)
        placed = jnp.concatenate(
            [jnp.where(place == at, source, zero) for at in range(members)], axis=1
        )
        if bit == 0:
            placed = lax.optimization_barrier(placed)
        others = in_place(zero, got, tables, place)
        source = placed + jnp.concatenate(
            [
                choose(place, [others[at ^ d] for d in range(members)])
                for at in range(members)
            ],
            axis=1,
        )

    far_vec = from_far(source)
    mirror = jnp.dot(source, matrix, preferred_element_type=jnp.float32)
    inside = row_idx + col_idx < rows
    far_vec = jnp.where(inside, far_vec, jnp.zeros_like(far_vec))
    far_vec = jnp.where(col_idx == 0, source, far_vec)
    gram = lax.dot_general(
        mirror,
        far_vec.astype(jnp.float32),
        (((1,), (1,)), ((), ())),
        precision=lax.Precision.HIGHEST,
    )
    plain = lax.dot_general(
        far_vec, matrix, (((1,), (1,)), ((), ())), preferred_element_type=jnp.float32
    )

    gram = gram + send(gram, lambda r, c: (r ^ 1, c))
    gram, plain = lax.optimization_barrier((gram, plain))
    arrived = to_far(mirror)
    for bit, members in groups_of(1, row_bits):
        place = (row_idx >> bit) % members
        tables = ROW_TABLES if members == 4 else ONE
        got = exchanged([gram] * len(tables), bit, tables, "row")
        if bit == 1:
            got[0], arrived = lax.optimization_barrier((got[0], arrived))
            arrived = jnp.where(row_idx >= col_idx, arrived, jnp.zeros_like(arrived))
            arrived = jnp.where(col_idx == 0, mirror, arrived)
            sums = plain + arrived
            other = send(sums, lambda r, c: (r ^ 1, c))
        gram = tree_sum(in_place(gram, held(got, ROW_ORDER), tables, place))

    gram = jnp.pad(gram, ((0, 0), (0, SUB - vectors)))
    mate = other
    for bit, members in reversed(groups_of(0, col_bits)):
        place = (col_idx >> bit) % members
        tables = SUM_TABLES if members == 4 else ONE
        own_pieces = jnp.split(sums, members, axis=1)
        mate_pieces = jnp.split(mate, members, axis=1)

        def message(to, first, second):
            blocks = [choose(to, first), choose(to, second), gram]
            return jnp.concatenate(blocks if bit else [blocks[0], gram], axis=1)

        given = [
            message(
                place,
                [mate_pieces[to] for to in table],
                [own_pieces[to] for to in table],
            )
            for table in tables
        ]
        own = message(place, own_pieces, mate_pieces)
        got = held(exchanged(given, bit, tables, "cross"), SUM_ORDER)
        both = tree_sum(in_place(own, got, tables, place))
        piece = own_pieces[0].shape[1]
        sums, mate, gram = both[:, :piece], both[:, piece:-SUB], both[:, -SUB:]

    return pl.pallas_call(
        functools.partial(write_results, 1.0 / (width * rows) ** 0.5),
        out_shape=(
            jax.ShapeDtypeStruct(lanczos_block.shape, jnp.float32),
            jax.ShapeDtypeStruct((vectors, vectors), jnp.float32),
        ),
        in_specs=[pl.BlockSpec(memory_space=pltpu.VMEM)],
        out_specs=(pl.BlockSpec(memory_space=pltpu.VMEM),) * 2,
        compiler_params=pltpu.CompilerParams(vmem_limit_bytes=1 << 20),
    )(both)


def solution(mesh):
    placed = (P("row", "col"), P("row", "col", None, None), P(None, ("row", "col")))
    return jax.shard_map(
        on_device,
        mesh=mesh,
        in_specs=placed,
        out_specs=(P(None, ("row", "col")), P()),
        check_vma=False,
    )
```

```python
import functools

import jax
import jax.numpy as jnp
from jax import lax
from jax.experimental import pallas as pl
from jax.experimental.pallas import tpu as pltpu
from jax.sharding import PartitionSpec as P

SUB = 128
AXES = ("row", "col")
ONE = ((1, 0),)
ROW_TABLES = ((2, 1, 0, 3), (1, 2, 3, 0), (3, 0, 1, 2), (0, 3, 2, 1))
ROW_ORDER = (0, 3, 1, 2)
GATHER_TABLES = ((2, 3, 0, 1), (0, 1, 3, 2), (3, 2, 1, 0), (1, 0, 2, 3))
GATHER_CROSS = (0, 0, 1, 1)
GATHER_ORDER = (0, 1, 2, 3)
SUM_TABLES = ((2, 1, 3, 0), (1, 0, 2, 3), (3, 2, 0, 1), (0, 3, 1, 2))
SUM_ORDER = (0, 1, 2, 3)


def send(block, target):
    rows, cols = lax.axis_size("row"), lax.axis_size("col")
    pairs = []
    for r in range(rows):
        for c in range(cols):
            to_row, to_col = target(r, c)
            pairs.append((r * cols + c, (to_row % rows) * cols + to_col))
    return lax.ppermute(block, AXES, pairs)


def moved(index, bit, table):
    size = len(table) - 1
    return index & ~(size << bit) | table[index >> bit & size] << bit


def exchanged(blocks, bit, tables, axis):
    if axis == "row":
        goes = [lambda r, c, t=t: (moved(r, bit, t) ^ 1, c) for t in tables]
    elif axis == "cross":
        goes = [lambda r, c, t=t: (r ^ 1, moved(c, bit, t)) for t in tables]
    else:
        goes = [
            lambda r, c, t=t, x=x: (
                r ^ (x or moved(c, bit, t) == c),
                moved(c, bit, t),
            )
            for t, x in zip(tables, GATHER_CROSS)
        ]
    return [send(block, to) for block, to in zip(blocks, goes)]


def held(blocks, order):
    if len(blocks) != len(order):
        return blocks
    kept = lax.optimization_barrier(tuple(blocks[k] for k in order))
    return [kept[order.index(k)] for k in range(len(blocks))]


def from_far(block):
    return send(block, lambda r, c: (r - c if c else r ^ 1, c))


def to_far(block):
    return send(block, lambda r, c: (r + c if c else r ^ 1, c))


def groups_of(first, last):
    return [(bit, 4 if bit + 1 < last else 2) for bit in range(first, last, 2)]


def choose(place, blocks):
    chosen = blocks[-1]
    for k in reversed(range(len(blocks) - 1)):
        chosen = jnp.where(place == k, blocks[k], chosen)
    return chosen


def in_place(own, got, tables, place):
    members = len(tables[0])

    def source(d, k):
        return next(g for g, t in zip(got, tables) if t[d ^ k] == d)

    return [own] + [
        choose(place, [source(d, k) for d in range(members)]) for k in range(1, members)
    ]


def tree_sum(blocks):
    while len(blocks) > 1:
        blocks = [a + b for a, b in zip(blocks[::2], blocks[1::2])]
    return blocks[0]


def write_results(scale, both_ref, product_ref, projected_ref):
    vectors = projected_ref.shape[0]
    product_ref[...] = both_ref[:, :-SUB]
    gram = both_ref[:, -SUB:]
    square = jnp.concatenate([gram, jnp.zeros((SUB - vectors, SUB), jnp.float32)])
    gram = gram + square.T[:vectors]
    projected_ref[...] = (gram * scale)[:, :vectors]


def on_device(tiles, block_map, lanczos_block):
    width = tiles.shape[0]
    vectors = lanczos_block.shape[0]
    parts = width // SUB
    rows, cols = lax.axis_size("row"), lax.axis_size("col")
    row_idx = lax.axis_index("row")
    col_idx = lax.axis_index("col")
    row_bits, col_bits = rows.bit_length() - 1, cols.bit_length() - 1

    source = lanczos_block
    for bit, members in groups_of(0, col_bits):
        place = (col_idx >> bit) % members
        tables = GATHER_TABLES if members == 4 else ONE
        mate = send(source, lambda r, c: (r ^ 1, c))
        given = [source] * len(tables)
        if bit == 0:
            mate, source, block_map = lax.optimization_barrier(
                (mate, source, block_map)
            )
        given = [mate if x else block for block, x in zip(given, GATHER_CROSS)]
        got = held(exchanged(given, bit, tables, "col"), GATHER_ORDER)
        zero = jnp.zeros_like(source)
        placed = jnp.concatenate(
            [jnp.where(place == at, source, zero) for at in range(members)], axis=1
        )
        if bit == 0:
            placed = lax.optimization_barrier(placed)
        others = in_place(zero, got, tables, place)
        source = placed + jnp.concatenate(
            [
                choose(place, [others[at ^ d] for d in range(members)])
                for at in range(members)
            ],
            axis=1,
        )

    keep = block_map[0, 0].astype(jnp.bfloat16)
    matrix = (tiles.reshape(parts, SUB, parts, SUB) * keep[:, None, :, None]).reshape(
        width, width
    )

    far_vec = from_far(source)
    mirror = jnp.dot(source, matrix, preferred_element_type=jnp.float32)
    inside = row_idx + col_idx < rows
    far_vec = jnp.where(inside, far_vec, jnp.zeros_like(far_vec))
    far_vec = jnp.where(col_idx == 0, source, far_vec)
    gram = lax.dot_general(
        mirror,
        far_vec.astype(jnp.float32),
        (((1,), (1,)), ((), ())),
        precision=lax.Precision.HIGHEST,
    )
    plain = lax.dot_general(
        far_vec, matrix, (((1,), (1,)), ((), ())), preferred_element_type=jnp.float32
    )

    gram = gram + send(gram, lambda r, c: (r ^ 1, c))
    gram, plain = lax.optimization_barrier((gram, plain))
    arrived = to_far(mirror)
    for bit, members in groups_of(1, row_bits):
        place = (row_idx >> bit) % members
        tables = ROW_TABLES if members == 4 else ONE
        got = exchanged([gram] * len(tables), bit, tables, "row")
        if bit == 1:
            got[0], arrived = lax.optimization_barrier((got[0], arrived))
            arrived = jnp.where(row_idx >= col_idx, arrived, jnp.zeros_like(arrived))
            arrived = jnp.where(col_idx == 0, mirror, arrived)
            sums = plain + arrived
            other = send(sums, lambda r, c: (r ^ 1, c))
        gram = tree_sum(in_place(gram, held(got, ROW_ORDER), tables, place))

    gram = jnp.pad(gram, ((0, 0), (0, SUB - vectors)))
    mate = other
    for bit, members in reversed(groups_of(0, col_bits)):
        place = (col_idx >> bit) % members
        tables = SUM_TABLES if members == 4 else ONE
        own_pieces = jnp.split(sums, members, axis=1)
        mate_pieces = jnp.split(mate, members, axis=1)

        def message(to, first, second):
            blocks = [choose(to, first), choose(to, second), gram]
            return jnp.concatenate(blocks if bit else [blocks[0], gram], axis=1)

        given = [
            message(
                place,
                [mate_pieces[to] for to in table],
                [own_pieces[to] for to in table],
            )
            for table in tables
        ]
        own = message(place, own_pieces, mate_pieces)
        got = held(exchanged(given, bit, tables, "cross"), SUM_ORDER)
        both = tree_sum(in_place(own, got, tables, place))
        piece = own_pieces[0].shape[1]
        sums, mate, gram = both[:, :piece], both[:, piece:-SUB], both[:, -SUB:]

    return pl.pallas_call(
        functools.partial(write_results, 1.0 / (width * rows) ** 0.5),
        out_shape=(
            jax.ShapeDtypeStruct(lanczos_block.shape, jnp.float32),
            jax.ShapeDtypeStruct((vectors, vectors), jnp.float32),
        ),
        in_specs=[pl.BlockSpec(memory_space=pltpu.VMEM)],
        out_specs=(pl.BlockSpec(memory_space=pltpu.VMEM),) * 2,
        compiler_params=pltpu.CompilerParams(vmem_limit_bytes=1 << 20),
    )(both)


def solution(mesh):
    placed = (P("row", "col"), P("row", "col", None, None), P(None, ("row", "col")))
    return jax.shard_map(
        on_device,
        mesh=mesh,
        in_specs=placed,
        out_specs=(P(None, ("row", "col")), P()),
        check_vma=False,
    )
```

```python
import functools

import jax
import jax.numpy as jnp
from jax import lax
from jax.experimental import pallas as pl
from jax.experimental.pallas import tpu as pltpu
from jax.sharding import PartitionSpec as P

SUB = 128
AXES = ("row", "col")
ONE = ((1, 0),)
ROW_TABLES = ((2, 1, 0, 3), (1, 2, 3, 0), (3, 0, 1, 2), (0, 3, 2, 1))
ROW_ORDER = (0, 1, 2, 3)
GATHER_TABLES = ((2, 3, 0, 1), (0, 1, 3, 2), (3, 2, 1, 0), (1, 0, 2, 3))
GATHER_CROSS = (0, 0, 1, 1)
GATHER_ORDER = (0, 1, 2, 3)
SUM_TABLES = ((2, 1, 3, 0), (1, 0, 2, 3), (3, 2, 0, 1), (0, 3, 1, 2))
SUM_ORDER = (0, 1, 2, 3)


def send(block, target):
    rows, cols = lax.axis_size("row"), lax.axis_size("col")
    pairs = []
    for r in range(rows):
        for c in range(cols):
            to_row, to_col = target(r, c)
            pairs.append((r * cols + c, (to_row % rows) * cols + to_col))
    return lax.ppermute(block, AXES, pairs)


def moved(index, bit, table):
    size = len(table) - 1
    return index & ~(size << bit) | table[index >> bit & size] << bit


def exchanged(blocks, bit, tables, axis):
    if axis == "row":
        goes = [lambda r, c, t=t: (moved(r, bit, t) ^ 1, c) for t in tables]
    elif axis == "cross":
        goes = [lambda r, c, t=t: (r ^ 1, moved(c, bit, t)) for t in tables]
    else:
        goes = [
            lambda r, c, t=t, x=x: (
                r ^ (x or moved(c, bit, t) == c),
                moved(c, bit, t),
            )
            for t, x in zip(tables, GATHER_CROSS)
        ]
    return [send(block, to) for block, to in zip(blocks, goes)]


def held(blocks, order):
    if len(blocks) != len(order):
        return blocks
    kept = lax.optimization_barrier(tuple(blocks[k] for k in order))
    return [kept[order.index(k)] for k in range(len(blocks))]


def from_far(block):
    return send(block, lambda r, c: (r - c if c else r ^ 1, c))


def to_far(block):
    return send(block, lambda r, c: (r + c if c else r ^ 1, c))


def groups_of(first, last):
    return [(bit, 4 if bit + 1 < last else 2) for bit in range(first, last, 2)]


def choose(place, blocks):
    chosen = blocks[-1]
    for k in reversed(range(len(blocks) - 1)):
        chosen = jnp.where(place == k, blocks[k], chosen)
    return chosen


def in_place(own, got, tables, place):
    members = len(tables[0])

    def source(d, k):
        return next(g for g, t in zip(got, tables) if t[d ^ k] == d)

    return [own] + [
        choose(place, [source(d, k) for d in range(members)]) for k in range(1, members)
    ]


def tree_sum(blocks):
    while len(blocks) > 1:
        blocks = [a + b for a, b in zip(blocks[::2], blocks[1::2])]
    return blocks[0]


def write_results(scale, both_ref, product_ref, projected_ref):
    vectors = projected_ref.shape[0]
    product_ref[...] = both_ref[:, :-SUB]
    gram = both_ref[:, -SUB:]
    square = jnp.concatenate([gram, jnp.zeros((SUB - vectors, SUB), jnp.float32)])
    gram = gram + square.T[:vectors]
    projected_ref[...] = (gram * scale)[:, :vectors]


def on_device(tiles, block_map, lanczos_block):
    width = tiles.shape[0]
    vectors = lanczos_block.shape[0]
    parts = width // SUB
    rows, cols = lax.axis_size("row"), lax.axis_size("col")
    row_idx = lax.axis_index("row")
    col_idx = lax.axis_index("col")
    row_bits, col_bits = rows.bit_length() - 1, cols.bit_length() - 1

    source = lanczos_block
    for bit, members in groups_of(0, col_bits):
        place = (col_idx >> bit) % members
        tables = GATHER_TABLES if members == 4 else ONE
        mate = send(source, lambda r, c: (r ^ 1, c))
        given = [source] * len(tables)
        if bit == 0:
            mate, source, block_map = lax.optimization_barrier(
                (mate, source, block_map)
            )
        given = [mate if x else block for block, x in zip(given, GATHER_CROSS)]
        got = held(exchanged(given, bit, tables, "col"), GATHER_ORDER)
        zero = jnp.zeros_like(source)
        placed = jnp.concatenate(
            [jnp.where(place == at, source, zero) for at in range(members)], axis=1
        )
        if bit == 0:
            placed = lax.optimization_barrier(placed)
        others = in_place(zero, got, tables, place)
        source = placed + jnp.concatenate(
            [
                choose(place, [others[at ^ d] for d in range(members)])
                for at in range(members)
            ],
            axis=1,
        )

    keep = block_map[0, 0].astype(jnp.bfloat16)
    matrix = (tiles.reshape(parts, SUB, parts, SUB) * keep[:, None, :, None]).reshape(
        width, width
    )

    far_vec = from_far(source)
    mirror = jnp.dot(source, matrix, preferred_element_type=jnp.float32)
    inside = row_idx + col_idx < rows
    far_vec = jnp.where(inside, far_vec, jnp.zeros_like(far_vec))
    far_vec = jnp.where(col_idx == 0, source, far_vec)
    gram = lax.dot_general(
        mirror,
        far_vec.astype(jnp.float32),
        (((1,), (1,)), ((), ())),
        precision=lax.Precision.HIGHEST,
    )
    plain = lax.dot_general(
        far_vec, matrix, (((1,), (1,)), ((), ())), preferred_element_type=jnp.float32
    )

    mate_gram = send(gram, lambda r, c: (r ^ 1, c))
    arrived = to_far(mirror)
    for bit, members in groups_of(1, row_bits):
        place = (row_idx >> bit) % members
        tables = ROW_TABLES if members == 4 else ONE
        early = members == 4 and bit == 1
        if early:
            first = exchanged([gram], bit, tables[:1], "row")[0]
        if bit == 1:
            gram = gram + mate_gram
            plain, gram = lax.optimization_barrier((plain, gram))
        if early:
            first, arrived = lax.optimization_barrier((first, arrived))
            last = jnp.where(place % 2 == 0, first, gram)
            got = exchanged([gram, gram, last], bit, tables[1:], "row")
            got = [first + got[2]] + got
        else:
            got = exchanged([gram] * len(tables), bit, tables, "row")
        if bit == 1:
            if not early:
                got[0], arrived = lax.optimization_barrier((got[0], arrived))
            arrived = jnp.where(row_idx >= col_idx, arrived, jnp.zeros_like(arrived))
            arrived = jnp.where(col_idx == 0, mirror, arrived)
            sums = plain + arrived
            other = send(sums, lambda r, c: (r ^ 1, c))
        gram = tree_sum(in_place(gram, held(got, ROW_ORDER), tables, place))

    gram = jnp.pad(gram, ((0, 0), (0, SUB - vectors)))
    mate = other
    for bit, members in reversed(groups_of(0, col_bits)):
        place = (col_idx >> bit) % members
        tables = SUM_TABLES if members == 4 else ONE
        own_pieces = jnp.split(sums, members, axis=1)
        mate_pieces = jnp.split(mate, members, axis=1)

        def message(to, first, second):
            blocks = [choose(to, first), choose(to, second), gram]
            return jnp.concatenate(blocks if bit else [blocks[0], gram], axis=1)

        given = [
            message(
                place,
                [mate_pieces[to] for to in table],
                [own_pieces[to] for to in table],
            )
            for table in tables
        ]
        own = message(place, own_pieces, mate_pieces)
        got = held(exchanged(given, bit, tables, "cross"), SUM_ORDER)
        both = tree_sum(in_place(own, got, tables, place))
        piece = own_pieces[0].shape[1]
        sums, mate, gram = both[:, :piece], both[:, piece:-SUB], both[:, -SUB:]

    return pl.pallas_call(
        functools.partial(write_results, 1.0 / (width * rows) ** 0.5),
        out_shape=(
            jax.ShapeDtypeStruct(lanczos_block.shape, jnp.float32),
            jax.ShapeDtypeStruct((vectors, vectors), jnp.float32),
        ),
        in_specs=[pl.BlockSpec(memory_space=pltpu.VMEM)],
        out_specs=(pl.BlockSpec(memory_space=pltpu.VMEM),) * 2,
        compiler_params=pltpu.CompilerParams(vmem_limit_bytes=1 << 20),
    )(both)


def solution(mesh):
    placed = (P("row", "col"), P("row", "col", None, None), P(None, ("row", "col")))
    return jax.shard_map(
        on_device,
        mesh=mesh,
        in_specs=placed,
        out_specs=(P(None, ("row", "col")), P()),
        check_vma=False,
    )
```

```python
import functools

import jax
import jax.numpy as jnp
from jax import lax
from jax.experimental import pallas as pl
from jax.experimental.pallas import tpu as pltpu
from jax.sharding import PartitionSpec as P

SUB = 128
AXES = ("row", "col")
ONE = ((1, 0),)
ROW_TABLES = ((2, 1, 0, 3), (1, 2, 3, 0), (3, 0, 1, 2), (0, 3, 2, 1))
ROW_ORDER = (0, 1, 2, 3)
GATHER_TABLES = ((2, 3, 0, 1), (0, 1, 3, 2), (3, 2, 1, 0), (1, 0, 2, 3))
GATHER_CROSS = (0, 0, 1, 1)
GATHER_ORDER = (0, 1, 2, 3)
SUM_TABLES = ((2, 1, 3, 0), (1, 0, 2, 3), (3, 2, 0, 1), (0, 3, 1, 2))
SUM_ORDER = (0, 1, 2, 3)


def send(block, target):
    rows, cols = lax.axis_size("row"), lax.axis_size("col")
    pairs = []
    for r in range(rows):
        for c in range(cols):
            to_row, to_col = target(r, c)
            pairs.append((r * cols + c, (to_row % rows) * cols + to_col))
    return lax.ppermute(block, AXES, pairs)


def moved(index, bit, table):
    size = len(table) - 1
    return index & ~(size << bit) | table[index >> bit & size] << bit


def exchanged(blocks, bit, tables, axis):
    if axis == "row":
        goes = [lambda r, c, t=t: (moved(r, bit, t) ^ 1, c) for t in tables]
    elif axis == "cross":
        goes = [lambda r, c, t=t: (r ^ 1, moved(c, bit, t)) for t in tables]
    else:
        goes = [
            lambda r, c, t=t, x=x: (
                r ^ (x or moved(c, bit, t) == c),
                moved(c, bit, t),
            )
            for t, x in zip(tables, GATHER_CROSS)
        ]
    return [send(block, to) for block, to in zip(blocks, goes)]


def held(blocks, order):
    if len(blocks) != len(order):
        return blocks
    kept = lax.optimization_barrier(tuple(blocks[k] for k in order))
    return [kept[order.index(k)] for k in range(len(blocks))]


def from_far(block):
    return send(block, lambda r, c: (r - c if c else r ^ 1, c))


def to_far(block):
    return send(block, lambda r, c: (r + c if c else r ^ 1, c))


def groups_of(first, last):
    return [(bit, 4 if bit + 1 < last else 2) for bit in range(first, last, 2)]


def choose(place, blocks):
    chosen = blocks[-1]
    for k in reversed(range(len(blocks) - 1)):
        chosen = jnp.where(place == k, blocks[k], chosen)
    return chosen


def in_place(own, got, tables, place):
    members = len(tables[0])

    def source(d, k):
        return next(g for g, t in zip(got, tables) if t[d ^ k] == d)

    return [own] + [
        choose(place, [source(d, k) for d in range(members)]) for k in range(1, members)
    ]


def tree_sum(blocks):
    while len(blocks) > 1:
        blocks = [a + b for a, b in zip(blocks[::2], blocks[1::2])]
    return blocks[0]


def write_results(scale, *refs):
    product_ref, projected_ref = refs[-2:]
    both = tree_sum([ref[...] for ref in refs[:-2]])
    vectors = projected_ref.shape[0]
    product_ref[...] = both[:, :-SUB]
    gram = both[:, -SUB:]
    square = jnp.concatenate([gram, jnp.zeros((SUB - vectors, SUB), jnp.float32)])
    gram = gram + square.T[:vectors]
    projected_ref[...] = (gram * scale)[:, :vectors]


def on_device(tiles, block_map, lanczos_block):
    width = tiles.shape[0]
    vectors = lanczos_block.shape[0]
    parts = width // SUB
    rows, cols = lax.axis_size("row"), lax.axis_size("col")
    row_idx = lax.axis_index("row")
    col_idx = lax.axis_index("col")
    row_bits, col_bits = rows.bit_length() - 1, cols.bit_length() - 1

    source = lanczos_block
    for bit, members in groups_of(0, col_bits):
        place = (col_idx >> bit) % members
        tables = GATHER_TABLES if members == 4 else ONE
        mate = send(source, lambda r, c: (r ^ 1, c))
        given = [source] * len(tables)
        if bit == 0:
            mate, source, block_map = lax.optimization_barrier(
                (mate, source, block_map)
            )
        given = [mate if x else block for block, x in zip(given, GATHER_CROSS)]
        got = held(exchanged(given, bit, tables, "col"), GATHER_ORDER)
        zero = jnp.zeros_like(source)
        placed = jnp.concatenate(
            [jnp.where(place == at, source, zero) for at in range(members)], axis=1
        )
        if bit == 0:
            placed = lax.optimization_barrier(placed)
        others = in_place(zero, got, tables, place)
        source = placed + jnp.concatenate(
            [
                choose(place, [others[at ^ d] for d in range(members)])
                for at in range(members)
            ],
            axis=1,
        )

    keep = block_map[0, 0].astype(jnp.bfloat16)
    matrix = (tiles.reshape(parts, SUB, parts, SUB) * keep[:, None, :, None]).reshape(
        width, width
    )

    far_vec = from_far(source)
    mirror = jnp.dot(source, matrix, preferred_element_type=jnp.float32)
    inside = row_idx + col_idx < rows
    far_vec = jnp.where(inside, far_vec, jnp.zeros_like(far_vec))
    far_vec = jnp.where(col_idx == 0, source, far_vec)
    gram = lax.dot_general(
        mirror,
        far_vec.astype(jnp.float32),
        (((1,), (1,)), ((), ())),
        precision=lax.Precision.HIGHEST,
    )
    plain = lax.dot_general(
        far_vec, matrix, (((1,), (1,)), ((), ())), preferred_element_type=jnp.float32
    )

    mate_gram = send(gram, lambda r, c: (r ^ 1, c))
    arrived = to_far(mirror)
    for bit, members in groups_of(1, row_bits):
        place = (row_idx >> bit) % members
        tables = ROW_TABLES if members == 4 else ONE
        early = members == 4 and bit == 1
        if early:
            first = exchanged([gram], bit, tables[:1], "row")[0]
        if bit == 1:
            gram = gram + mate_gram
            plain, gram = lax.optimization_barrier((plain, gram))
        if early:
            first, arrived = lax.optimization_barrier((first, arrived))
            last = jnp.where(place % 2 == 0, first, gram)
            got = exchanged([gram, gram, last], bit, tables[1:], "row")
            got = [first + got[2]] + got
        else:
            got = exchanged([gram] * len(tables), bit, tables, "row")
        if bit == 1:
            if not early:
                got[0], arrived = lax.optimization_barrier((got[0], arrived))
            arrived = jnp.where(row_idx >= col_idx, arrived, jnp.zeros_like(arrived))
            arrived = jnp.where(col_idx == 0, mirror, arrived)
            sums = plain + arrived
            other = send(sums, lambda r, c: (r ^ 1, c))
        gram = tree_sum(in_place(gram, held(got, ROW_ORDER), tables, place))

    gram = jnp.pad(gram, ((0, 0), (0, SUB - vectors)))
    mate = other
    for bit, members in reversed(groups_of(0, col_bits)):
        place = (col_idx >> bit) % members
        tables = SUM_TABLES if members == 4 else ONE
        own_pieces = jnp.split(sums, members, axis=1)
        mate_pieces = jnp.split(mate, members, axis=1)

        def message(to, first, second):
            blocks = [choose(to, first), choose(to, second), gram]
            return jnp.concatenate(blocks if bit else [blocks[0], gram], axis=1)

        given = [
            message(
                place,
                [mate_pieces[to] for to in table],
                [own_pieces[to] for to in table],
            )
            for table in tables
        ]
        own = message(place, own_pieces, mate_pieces)
        got = held(exchanged(given, bit, tables, "cross"), SUM_ORDER)
        terms = in_place(own, got, tables, place)
        if not bit:
            break
        both = tree_sum(terms)
        piece = own_pieces[0].shape[1]
        sums, mate, gram = both[:, :piece], both[:, piece:-SUB], both[:, -SUB:]

    return pl.pallas_call(
        functools.partial(write_results, 1.0 / (width * rows) ** 0.5),
        out_shape=(
            jax.ShapeDtypeStruct(lanczos_block.shape, jnp.float32),
            jax.ShapeDtypeStruct((vectors, vectors), jnp.float32),
        ),
        in_specs=[pl.BlockSpec(memory_space=pltpu.VMEM)] * len(terms),
        out_specs=(pl.BlockSpec(memory_space=pltpu.VMEM),) * 2,
        compiler_params=pltpu.CompilerParams(vmem_limit_bytes=1 << 20),
    )(*terms)


def solution(mesh):
    placed = (P("row", "col"), P("row", "col", None, None), P(None, ("row", "col")))
    return jax.shard_map(
        on_device,
        mesh=mesh,
        in_specs=placed,
        out_specs=(P(None, ("row", "col")), P()),
        check_vma=False,
    )
```

```python
import functools

import jax
import jax.numpy as jnp
from jax import lax
from jax.experimental import pallas as pl
from jax.experimental.pallas import tpu as pltpu
from jax.sharding import PartitionSpec as P

SUB = 128
AXES = ("row", "col")
ONE = ((1, 0),)
ROW_TABLES = ((2, 1, 0, 3), (1, 2, 3, 0), (3, 0, 1, 2), (0, 3, 2, 1))
ROW_ORDER = (0, 1, 2, 3)
GATHER_TABLES = ((2, 3, 0, 1), (0, 1, 3, 2), (3, 2, 1, 0), (1, 0, 2, 3))
GATHER_CROSS = (0, 0, 1, 1)
GATHER_ORDER = (0, 1, 2, 3)
SUM_TABLES = ((2, 1, 3, 0), (1, 0, 2, 3), (3, 2, 0, 1), (0, 3, 1, 2))
SUM_CROSS = (1, 0, 1, 1)
SUM_ORDER = (0, 1, 2, 3)


def send(block, target):
    rows, cols = lax.axis_size("row"), lax.axis_size("col")
    pairs = []
    for r in range(rows):
        for c in range(cols):
            to_row, to_col = target(r, c)
            pairs.append((r * cols + c, (to_row % rows) * cols + to_col))
    return lax.ppermute(block, AXES, pairs)


def moved(index, bit, table):
    size = len(table) - 1
    return index & ~(size << bit) | table[index >> bit & size] << bit


def exchanged(blocks, bit, tables, axis):
    if axis == "row":
        goes = [lambda r, c, t=t: (moved(r, bit, t) ^ 1, c) for t in tables]
    elif axis == "cross":
        goes = [
            lambda r, c, t=t, x=x: (
                r ^ (x or moved(c, bit, t) == c),
                moved(c, bit, t),
            )
            for t, x in zip(tables, SUM_CROSS)
        ]
    else:
        goes = [
            lambda r, c, t=t, x=x: (
                r ^ (x or moved(c, bit, t) == c),
                moved(c, bit, t),
            )
            for t, x in zip(tables, GATHER_CROSS)
        ]
    return [send(block, to) for block, to in zip(blocks, goes)]


def held(blocks, order):
    if len(blocks) != len(order):
        return blocks
    kept = lax.optimization_barrier(tuple(blocks[k] for k in order))
    return [kept[order.index(k)] for k in range(len(blocks))]


def from_far(block):
    return send(block, lambda r, c: (r - c if c else r ^ 1, c))


def to_far(block):
    return send(block, lambda r, c: (r + c if c else r ^ 1, c))


def groups_of(first, last):
    return [(bit, 4 if bit + 1 < last else 2) for bit in range(first, last, 2)]


def choose(place, blocks):
    chosen = blocks[-1]
    for k in reversed(range(len(blocks) - 1)):
        chosen = jnp.where(place == k, blocks[k], chosen)
    return chosen


def in_place(own, got, tables, place):
    members = len(tables[0])

    def source(d, k):
        return next(g for g, t in zip(got, tables) if t[d ^ k] == d)

    return [own] + [
        choose(place, [source(d, k) for d in range(members)]) for k in range(1, members)
    ]


def tree_sum(blocks):
    while len(blocks) > 1:
        blocks = [a + b for a, b in zip(blocks[::2], blocks[1::2])]
    return blocks[0]


def write_results(scale, *refs):
    product_ref, projected_ref = refs[-2:]
    both = tree_sum([ref[...] for ref in refs[:-2]])
    vectors = projected_ref.shape[0]
    product_ref[...] = both[:, :-SUB]
    gram = both[:, -SUB:]
    square = jnp.concatenate([gram, jnp.zeros((SUB - vectors, SUB), jnp.float32)])
    gram = gram + square.T[:vectors]
    projected_ref[...] = (gram * scale)[:, :vectors]


def on_device(tiles, block_map, lanczos_block):
    width = tiles.shape[0]
    vectors = lanczos_block.shape[0]
    parts = width // SUB
    rows, cols = lax.axis_size("row"), lax.axis_size("col")
    row_idx = lax.axis_index("row")
    col_idx = lax.axis_index("col")
    row_bits, col_bits = rows.bit_length() - 1, cols.bit_length() - 1

    source = lanczos_block
    for bit, members in groups_of(0, col_bits):
        place = (col_idx >> bit) % members
        tables = GATHER_TABLES if members == 4 else ONE
        mate = send(source, lambda r, c: (r ^ 1, c))
        given = [source] * len(tables)
        if bit == 0:
            mate, source, block_map = lax.optimization_barrier(
                (mate, source, block_map)
            )
        given = [mate if x else block for block, x in zip(given, GATHER_CROSS)]
        got = held(exchanged(given, bit, tables, "col"), GATHER_ORDER)
        zero = jnp.zeros_like(source)
        placed = jnp.concatenate(
            [jnp.where(place == at, source, zero) for at in range(members)], axis=1
        )
        if bit == 0:
            placed = lax.optimization_barrier(placed)
        others = in_place(zero, got, tables, place)
        source = placed + jnp.concatenate(
            [
                choose(place, [others[at ^ d] for d in range(members)])
                for at in range(members)
            ],
            axis=1,
        )

    keep = block_map[0, 0].astype(jnp.bfloat16)
    matrix = (tiles.reshape(parts, SUB, parts, SUB) * keep[:, None, :, None]).reshape(
        width, width
    )

    far_vec = from_far(source)
    mirror = jnp.dot(source, matrix, preferred_element_type=jnp.float32)
    inside = row_idx + col_idx < rows
    far_vec = jnp.where(inside, far_vec, jnp.zeros_like(far_vec))
    far_vec = jnp.where(col_idx == 0, source, far_vec)
    gram = lax.dot_general(
        mirror,
        far_vec.astype(jnp.float32),
        (((1,), (1,)), ((), ())),
        precision=lax.Precision.HIGHEST,
    )
    plain = lax.dot_general(
        far_vec, matrix, (((1,), (1,)), ((), ())), preferred_element_type=jnp.float32
    )

    mate_gram = send(gram, lambda r, c: (r ^ 1, c))
    arrived = to_far(mirror)
    for bit, members in groups_of(1, row_bits):
        place = (row_idx >> bit) % members
        tables = ROW_TABLES if members == 4 else ONE
        early = members == 4 and bit == 1
        if early:
            first = exchanged([gram], bit, tables[:1], "row")[0]
        if bit == 1:
            gram = gram + mate_gram
            plain, gram = lax.optimization_barrier((plain, gram))
        if early:
            first, arrived = lax.optimization_barrier((first, arrived))
            last = jnp.where(place % 2 == 0, first, gram)
            got = exchanged([gram, gram, last], bit, tables[1:], "row")
            got = [first + got[2]] + got
        else:
            got = exchanged([gram] * len(tables), bit, tables, "row")
        if bit == 1:
            if not early:
                got[0], arrived = lax.optimization_barrier((got[0], arrived))
            arrived = jnp.where(row_idx >= col_idx, arrived, jnp.zeros_like(arrived))
            arrived = jnp.where(col_idx == 0, mirror, arrived)
            sums = plain + arrived
            other = send(sums, lambda r, c: (r ^ 1, c))
        gram = tree_sum(in_place(gram, held(got, ROW_ORDER), tables, place))

    gram = jnp.pad(gram, ((0, 0), (0, SUB - vectors)))
    mate = other
    for bit, members in reversed(groups_of(0, col_bits)):
        place = (col_idx >> bit) % members
        tables = SUM_TABLES if members == 4 else ONE
        own_pieces = jnp.split(sums, members, axis=1)
        mate_pieces = jnp.split(mate, members, axis=1)

        def message(to, first, second):
            blocks = [choose(to, first), choose(to, second), gram]
            return jnp.concatenate(blocks if bit else [blocks[0], gram], axis=1)

        given = []
        for table, cross in zip(tables, SUM_CROSS):
            own_rows = [own_pieces[to] for to in table]
            mate_rows = [mate_pieces[to] for to in table]
            if cross:
                own_rows, mate_rows = mate_rows, own_rows
            given.append(message(place, own_rows, mate_rows))
        own = message(place, own_pieces, mate_pieces)
        got = held(exchanged(given, bit, tables, "cross"), SUM_ORDER)
        terms = in_place(own, got, tables, place)
        if not bit:
            break
        both = tree_sum(terms)
        piece = own_pieces[0].shape[1]
        sums, mate, gram = both[:, :piece], both[:, piece:-SUB], both[:, -SUB:]

    return pl.pallas_call(
        functools.partial(write_results, 1.0 / (width * rows) ** 0.5),
        out_shape=(
            jax.ShapeDtypeStruct(lanczos_block.shape, jnp.float32),
            jax.ShapeDtypeStruct((vectors, vectors), jnp.float32),
        ),
        in_specs=[pl.BlockSpec(memory_space=pltpu.VMEM)] * len(terms),
        out_specs=(pl.BlockSpec(memory_space=pltpu.VMEM),) * 2,
        compiler_params=pltpu.CompilerParams(vmem_limit_bytes=1 << 20),
    )(*terms)


def solution(mesh):
    placed = (P("row", "col"), P("row", "col", None, None), P(None, ("row", "col")))
    return jax.shard_map(
        on_device,
        mesh=mesh,
        in_specs=placed,
        out_specs=(P(None, ("row", "col")), P()),
        check_vma=False,
    )
```

```python
import functools

import jax
import jax.numpy as jnp
from jax import lax
from jax.experimental import pallas as pl
from jax.experimental.pallas import tpu as pltpu
from jax.sharding import PartitionSpec as P

SUB = 128
AXES = ("row", "col")
ONE = ((1, 0),)
ROW_TABLES = ((2, 1, 0, 3), (1, 2, 3, 0), (3, 0, 1, 2), (0, 3, 2, 1))
ROW_ORDER = (0, 1, 2, 3)
GATHER_TABLES = ((2, 3, 0, 1), (0, 1, 3, 2), (3, 2, 1, 0), (1, 0, 2, 3))
GATHER_CROSS = (0, 0, 1, 1)
GATHER_ORDER = (0, 1, 2, 3)
SUM_TABLES = ((2, 1, 3, 0), (1, 0, 2, 3), (3, 2, 0, 1), (0, 3, 1, 2))
SUM_CROSS = (1, 0, 1, 0)
SUM_ORDER = (0, 1, 2, 3)


def send(block, target):
    rows, cols = lax.axis_size("row"), lax.axis_size("col")
    pairs = []
    for r in range(rows):
        for c in range(cols):
            to_row, to_col = target(r, c)
            pairs.append((r * cols + c, (to_row % rows) * cols + to_col))
    return lax.ppermute(block, AXES, pairs)


def moved(index, bit, table):
    size = len(table) - 1
    return index & ~(size << bit) | table[index >> bit & size] << bit


def exchanged(blocks, bit, tables, axis):
    if axis == "row":
        goes = [lambda r, c, t=t: (moved(r, bit, t) ^ 1, c) for t in tables]
    elif axis == "cross":
        goes = [
            lambda r, c, t=t, x=x: (
                r ^ (x or moved(c, bit, t) == c),
                moved(c, bit, t),
            )
            for t, x in zip(tables, SUM_CROSS)
        ]
    else:
        goes = [
            lambda r, c, t=t, x=x: (
                r ^ (x or moved(c, bit, t) == c),
                moved(c, bit, t),
            )
            for t, x in zip(tables, GATHER_CROSS)
        ]
    return [send(block, to) for block, to in zip(blocks, goes)]


def held(blocks, order):
    if len(blocks) != len(order):
        return blocks
    kept = lax.optimization_barrier(tuple(blocks[k] for k in order))
    return [kept[order.index(k)] for k in range(len(blocks))]


def from_far(block):
    return send(block, lambda r, c: (r - c if c else r ^ 1, c))


def to_far(block):
    return send(block, lambda r, c: (r + c if c else r ^ 1, c))


def groups_of(first, last):
    return [(bit, 4 if bit + 1 < last else 2) for bit in range(first, last, 2)]


def choose(place, blocks):
    chosen = blocks[-1]
    for k in reversed(range(len(blocks) - 1)):
        chosen = jnp.where(place == k, blocks[k], chosen)
    return chosen


def in_place(own, got, tables, place):
    members = len(tables[0])

    def source(d, k):
        return next(g for g, t in zip(got, tables) if t[d ^ k] == d)

    return [own] + [
        choose(place, [source(d, k) for d in range(members)]) for k in range(1, members)
    ]


def tree_sum(blocks):
    while len(blocks) > 1:
        blocks = [a + b for a, b in zip(blocks[::2], blocks[1::2])]
    return blocks[0]


def write_results(scale, *refs):
    product_ref, projected_ref = refs[-2:]
    both = tree_sum([ref[...] for ref in refs[:-2]])
    vectors = projected_ref.shape[0]
    product_ref[...] = both[:, :-SUB]
    gram = both[:, -SUB:]
    square = jnp.concatenate([gram, jnp.zeros((SUB - vectors, SUB), jnp.float32)])
    gram = gram + square.T[:vectors]
    projected_ref[...] = (gram * scale)[:, :vectors]


def on_device(tiles, block_map, lanczos_block):
    width = tiles.shape[0]
    vectors = lanczos_block.shape[0]
    parts = width // SUB
    rows, cols = lax.axis_size("row"), lax.axis_size("col")
    row_idx = lax.axis_index("row")
    col_idx = lax.axis_index("col")
    row_bits, col_bits = rows.bit_length() - 1, cols.bit_length() - 1

    source = lanczos_block
    for bit, members in groups_of(0, col_bits):
        place = (col_idx >> bit) % members
        tables = GATHER_TABLES if members == 4 else ONE
        mate = send(source, lambda r, c: (r ^ 1, c))
        given = [source] * len(tables)
        if bit == 0:
            mate, source, block_map = lax.optimization_barrier(
                (mate, source, block_map)
            )
        given = [mate if x else block for block, x in zip(given, GATHER_CROSS)]
        got = held(exchanged(given, bit, tables, "col"), GATHER_ORDER)
        zero = jnp.zeros_like(source)
        placed = jnp.concatenate(
            [jnp.where(place == at, source, zero) for at in range(members)], axis=1
        )
        if bit == 0:
            placed = lax.optimization_barrier(placed)
        others = in_place(zero, got, tables, place)
        source = placed + jnp.concatenate(
            [
                choose(place, [others[at ^ d] for d in range(members)])
                for at in range(members)
            ],
            axis=1,
        )

    keep = block_map[0, 0].astype(jnp.bfloat16)
    matrix = (tiles.reshape(parts, SUB, parts, SUB) * keep[:, None, :, None]).reshape(
        width, width
    )

    far_vec = from_far(source)
    mirror = jnp.dot(source, matrix, preferred_element_type=jnp.float32)
    inside = row_idx + col_idx < rows
    far_vec = jnp.where(inside, far_vec, jnp.zeros_like(far_vec))
    far_vec = jnp.where(col_idx == 0, source, far_vec)
    gram = lax.dot_general(
        mirror,
        far_vec.astype(jnp.float32),
        (((1,), (1,)), ((), ())),
        precision=lax.Precision.HIGHEST,
    )
    plain = lax.dot_general(
        far_vec, matrix, (((1,), (1,)), ((), ())), preferred_element_type=jnp.float32
    )

    mate_gram = send(gram, lambda r, c: (r ^ 1, c))
    arrived = to_far(mirror)
    for bit, members in groups_of(1, row_bits):
        place = (row_idx >> bit) % members
        tables = ROW_TABLES if members == 4 else ONE
        early = members == 4 and bit == 1
        if early:
            first = exchanged([gram], bit, tables[:1], "row")[0]
        if bit == 1:
            gram = gram + mate_gram
            plain, gram = lax.optimization_barrier((plain, gram))
        if early:
            first, arrived = lax.optimization_barrier((first, arrived))
            last = jnp.where(place % 2 == 0, first, gram)
            got = exchanged([gram, gram, last], bit, tables[1:], "row")
            got = [first + got[2]] + got
        else:
            got = exchanged([gram] * len(tables), bit, tables, "row")
        if bit == 1:
            if not early:
                got[0], arrived = lax.optimization_barrier((got[0], arrived))
            arrived = jnp.where(row_idx >= col_idx, arrived, jnp.zeros_like(arrived))
            arrived = jnp.where(col_idx == 0, mirror, arrived)
            sums = plain + arrived
            other = send(sums, lambda r, c: (r ^ 1, c))
        gram = tree_sum(in_place(gram, held(got, ROW_ORDER), tables, place))

    gram = jnp.pad(gram, ((0, 0), (0, SUB - vectors)))
    mate = other
    for bit, members in reversed(groups_of(0, col_bits)):
        place = (col_idx >> bit) % members
        tables = SUM_TABLES if members == 4 else ONE
        own_pieces = jnp.split(sums, members, axis=1)
        mate_pieces = jnp.split(mate, members, axis=1)

        def message(to, first, second):
            blocks = [choose(to, first), choose(to, second), gram]
            return jnp.concatenate(blocks if bit else [blocks[0], gram], axis=1)

        given = []
        for table, cross in zip(tables, SUM_CROSS):
            own_rows = [own_pieces[to] for to in table]
            mate_rows = [mate_pieces[to] for to in table]
            if cross:
                own_rows, mate_rows = mate_rows, own_rows
            given.append(message(place, own_rows, mate_rows))
        own = message(place, own_pieces, mate_pieces)
        got = held(exchanged(given, bit, tables, "cross"), SUM_ORDER)
        terms = in_place(own, got, tables, place)
        if not bit:
            break
        both = tree_sum(terms)
        piece = own_pieces[0].shape[1]
        sums, mate, gram = both[:, :piece], both[:, piece:-SUB], both[:, -SUB:]

    return pl.pallas_call(
        functools.partial(write_results, 1.0 / (width * rows) ** 0.5),
        out_shape=(
            jax.ShapeDtypeStruct(lanczos_block.shape, jnp.float32),
            jax.ShapeDtypeStruct((vectors, vectors), jnp.float32),
        ),
        in_specs=[pl.BlockSpec(memory_space=pltpu.VMEM)] * len(terms),
        out_specs=(pl.BlockSpec(memory_space=pltpu.VMEM),) * 2,
        compiler_params=pltpu.CompilerParams(vmem_limit_bytes=1 << 20),
    )(*terms)


def solution(mesh):
    placed = (P("row", "col"), P("row", "col", None, None), P(None, ("row", "col")))
    return jax.shard_map(
        on_device,
        mesh=mesh,
        in_specs=placed,
        out_specs=(P(None, ("row", "col")), P()),
        check_vma=False,
    )
```
